32 devices in a mesh: groups: 2 (over y), row: 4 (over x, core), col: 4 (over z).
Axes of the slice: x: 2, y: 2, z: 4, core: 2. Of those that a mesh axis runs over, the one named last changes fastest.
Arguments:
- features: float32 [32, 65536], P(None, ('groups', 'row', 'col')), parts along dimension 1, may hold values from -6 to 6
- noise: float32 [65536], P(('groups', 'row', 'col')), parts along dimension 0, may hold values from 0.5 to 4
- solution: float32 [16, 65536], P(None, ('groups', 'row', 'col')), parts along dimension 1, may hold values from -6 to 6
- residual: float32 [16, 65536], P(None, ('groups', 'row', 'col')), parts along dimension 1, may hold values from -12 to 12
- direction: float32 [16, 65536], P(None, ('groups', 'row', 'col')), parts along dimension 1, may hold values from -12 to 12
- tile_rows: int32 [8, 4, 64], P(('groups', 'row'), 'col'), parts along dimension 0, may hold values from 0 to 15, as said below
- tile_cols: int32 [8, 4, 64], P(('groups', 'row'), 'col'), parts along dimension 0, may hold values from 0 to 15, as said below
- tile_count: int32 [8, 4], P(('groups', 'row'), 'col'), parts along dimension 0, may hold values from 1 to 64, as said below
Outputs:
- solution_next: float32 [16, 65536], P(None, ('groups', 'row', 'col')), parts along dimension 1
- residual_next: float32 [16, 65536], P(None, ('groups', 'row', 'col')), parts along dimension 1
- direction_next: float32 [16, 65536], P(None, ('groups', 'row', 'col')), parts along dimension 1
The draws below stay inside these ranges and needn't reach their ends.
There are 2 independent parts, one for each index of `groups`. The reference program is written for one: setup_inputs(seed, part) draws one part's arguments, and reference() takes and returns one part's arrays. A program takes and returns all parts, laid end to end along the dimension named above; each array names one. Nothing has to cross between parts.
Inputs may be any that keep to these rules, and one draw needn't show every extreme that they name: `tile_rows`: every listed slot names a tile with I <= J; the slots of one device name distinct tiles. `tile_cols`: see tile_rows. `tile_count`: some device of every problem lists 64 tiles.
All inputs are finite; a program needn't handle non-finite values.
Results may differ from the reference program's by a relative error of at most 0.0003.
Values sent between devices are 32-bit elements; how exact they have to be, the bound alone decides.
A program may use at most 64 MiB of HBM per device.

```python
import math
import jax
import jax.numpy as jnp
from jax import lax

FEAT = 32
RHS = 16
BLOCK = 512
BLK_DEV = 4
MAXT = 64
POINTS = 32768
N_ROW = 4
N_COL = 4


def tile_plan(key):
    folded = jax.random.fold_in(key, 7)
    key_count, key_rank, key_pick = jax.random.split(folded, 3)
    row_local = N_COL * BLK_DEV
    col_local = N_ROW * BLK_DEV
    pairs = row_local * col_local
    pair_ids = jnp.arange(pairs, dtype=jnp.int32)
    pair_rows = pair_ids // col_local
    pair_cols = pair_ids % col_local
    rank_row = jnp.arange(N_ROW, dtype=jnp.int32)[:, None, None]
    rank_col = jnp.arange(N_COL, dtype=jnp.int32)[None, :, None]
    big_rows = rank_row * row_local + pair_rows[None, None, :]
    big_cols = pair_cols[None, None, :] // BLK_DEV * row_local + rank_col * BLK_DEV + pair_cols[None, None, :] % BLK_DEV
    valid = big_rows <= big_cols
    chosen_col = jax.random.randint(key_pick, (), 0, N_COL)
    forced = (rank_row == 0) & (rank_col == chosen_col)
    first_pair = (pair_rows == row_local - 1) & (pair_cols == col_local - 1)
    second_pair = (pair_rows == 0) & (pair_cols == 0)
    levels = 2 ** 29 // pairs
    ranked = jax.random.randint(key_rank, (N_ROW, N_COL, pairs), 0, levels) * pairs + pair_ids[None, None, :]
    sort_key = jnp.where(valid, ranked, ranked + 2 ** 29)
    sort_key = jnp.where(forced & second_pair[None, None, :], -1, sort_key)
    sort_key = jnp.where(forced & first_pair[None, None, :], -2, sort_key)
    order = jnp.argsort(sort_key, axis=-1, stable=True)[:, :, :MAXT].astype(jnp.int32)
    row_slots = order // col_local
    col_slots = order % col_local
    valid_count = jnp.sum(valid.astype(jnp.int32), -1)
    drawn = jax.random.randint(key_count, (N_ROW, N_COL), max(1, MAXT // 8), MAXT + 1)
    totals = jnp.minimum(drawn, valid_count)
    totals = jnp.where(forced[:, :, 0], MAXT, totals).astype(jnp.int32)
    return (row_slots, col_slots, totals)


def draw_tile_rows(key, part):
    return tile_plan(key)[0]


def draw_tile_cols(key, part):
    return tile_plan(key)[1]


def draw_tile_count(key, part):
    return tile_plan(key)[2]


def rising_field(key):
    first = jax.random.fold_in(key, 0)
    spot = jnp.arange(POINTS, dtype=jnp.float32) / POINTS
    rising = 1.0 + 2.0 * spot
    field = jnp.clip(jax.random.normal(first, (RHS, POINTS), jnp.float32), -4.0, 4.0)
    return (field * rising[None, :]).astype(jnp.float32)


def draw_residual(key, part):
    return rising_field(jax.random.fold_in(key, 11))


def draw_direction(key, part):
    return rising_field(jax.random.fold_in(key, 12))


def block_levels(rng, shape, cuts, smallest, high):
    factor_of = 1.0
    for axis_at, shards_of in cuts:
        draws = jax.random.uniform(jax.random.fold_in(jax.random.fold_in(rng, 6), axis_at), (shards_of,), jnp.float32, smallest / len(cuts), high / len(cuts))
        factor_of = factor_of * jnp.repeat(jnp.exp(draws), shape[axis_at] // shards_of).reshape((-1,) + (1,) * (len(shape) - 1 - axis_at))
    return factor_of


def scatter_about(own_key, dims, scale, reach, cuts=(), held_as=jnp.bfloat16):
    entries = jax.random.normal(own_key, dims, jnp.float32) * scale
    if len(cuts) > 0:
        entries = block_levels(own_key, dims, cuts, -0.22, 0.18) * entries
    return jnp.clip(entries, min=-reach, max=reach).astype(held_as)


def setup_inputs(seed: int = 0, part: int = 0) -> dict:
    splits = jax.random.split(jax.random.key(seed), 9)
    part_splits = jax.random.split(jax.random.fold_in(splits[8], part), 9)
    return {
        "features": scatter_about(part_splits[0], (FEAT, POINTS), 1.0, 6.0, ((1, 16),), jnp.float32),
        "noise": jnp.clip(jnp.exp(math.log(4.0) - 2.0794415 * jax.random.uniform(part_splits[1], (POINTS,), jnp.float32) ** block_levels(part_splits[1], (POINTS,), ((0, 16),), -0.2, 0.2)), 0.5, 4.0),
        "solution": scatter_about(part_splits[2], (RHS, POINTS), 1.0, 6.0, ((1, 16),), jnp.float32),
        "residual": draw_residual(jax.random.fold_in(jax.random.fold_in(splits[8], part), 71), part),
        "direction": draw_direction(jax.random.fold_in(jax.random.fold_in(splits[8], part), 71), part),
        "tile_rows": draw_tile_rows(jax.random.fold_in(jax.random.fold_in(splits[8], part), 71), part),
        "tile_cols": draw_tile_cols(jax.random.fold_in(jax.random.fold_in(splits[8], part), 71), part),
        "tile_count": draw_tile_count(jax.random.fold_in(jax.random.fold_in(splits[8], part), 71), part),
    }


HIGH = lax.Precision.HIGHEST

def tile_kernel(row_points, col_points):
    inner = lax.dot_general(row_points.astype(jnp.float32), col_points.astype(jnp.float32), (((0,), (0,)), ((), ())), precision=HIGH, preferred_element_type=jnp.float32)
    row_norms = lax.optimization_barrier(jnp.sum(row_points * row_points, 0))
    col_norms = lax.optimization_barrier(jnp.sum(col_points * col_points, 0))
    dist_sq = jnp.maximum(row_norms[:, None] + col_norms[None, :] - 2.0 * inner, 0.0)
    radius = jnp.sqrt(dist_sq) / (1.5 * math.sqrt(row_points.shape[0]))
    inside = jnp.maximum(1.0 - radius, 0.0)
    return inside ** 4 * (4.0 * radius + 1.0)

def gram(left, right):
    return lax.dot_general(left.astype(jnp.float32), right.astype(jnp.float32), (((1,), (1,)), ((), ())), precision=HIGH, preferred_element_type=jnp.float32)

def symmetric(matrix):
    return 0.5 * (matrix + matrix.T)

def spd_solve(matrix, target):
    lower = jnp.linalg.cholesky(matrix)
    half_way = lax.linalg.triangular_solve(lower, target, left_side=True, lower=True)
    return lax.linalg.triangular_solve(lower, half_way, left_side=True, lower=True, transpose_a=True)

def apply_left(coeffs, field):
    return lax.dot_general(coeffs.astype(jnp.float32), field.astype(jnp.float32), (((0,), (0,)), ((), ())), precision=HIGH, preferred_element_type=jnp.float32)

def add_at(running, addend, start):
    axis_last = running.ndim - 1
    current = lax.dynamic_slice_in_dim(running, start, addend.shape[-1], axis_last)
    return lax.dynamic_update_slice_in_dim(running, current + addend, start, axis_last)

def reference(features, noise, solution, residual, direction, tile_rows, tile_cols, tile_count):
    span = N_COL * BLK_DEV
    total_slots = N_ROW * N_COL * MAXT
    slot_ids = jnp.arange(total_slots, dtype=jnp.int32)
    device_ids = slot_ids // MAXT
    within = slot_ids % MAXT
    rank_row = device_ids // N_COL
    rank_col = device_ids % N_COL
    flat_rows = tile_rows.reshape(-1).astype(jnp.int32)
    flat_cols = tile_cols.reshape(-1).astype(jnp.int32)
    used_flags = within < tile_count.reshape(-1).astype(jnp.int32)[device_ids]
    big_rows = rank_row * span + flat_rows
    big_cols = flat_cols // BLK_DEV * span + rank_col * BLK_DEV + flat_cols % BLK_DEV

    def keep_state(state):
        return state

    def one_tile(carried, item):
        big_i, big_j, used_flag = item

        def apply_tile(state):
            image, degree = state
            start_i = (big_i * BLOCK).astype(jnp.int32)
            start_j = (big_j * BLOCK).astype(jnp.int32)
            kernel = tile_kernel(lax.dynamic_slice_in_dim(features, start_i, BLOCK, 1), lax.dynamic_slice_in_dim(features, start_j, BLOCK, 1))
            mirror = (big_i != big_j).astype(jnp.float32)
            dir_rows = lax.dynamic_slice_in_dim(direction, start_i, BLOCK, 1)
            dir_cols = lax.dynamic_slice_in_dim(direction, start_j, BLOCK, 1)
            row_term = lax.dot_general(dir_cols.astype(jnp.float32), kernel.astype(jnp.float32), (((1,), (1,)), ((), ())), precision=HIGH, preferred_element_type=jnp.float32)
            col_term = lax.dot_general(dir_rows.astype(jnp.float32), kernel.astype(jnp.float32), (((1,), (0,)), ((), ())), precision=HIGH, preferred_element_type=jnp.float32) * mirror
            image = add_at(image, row_term, start_i)
            image = add_at(image, col_term, start_j)
            degree = add_at(degree, lax.optimization_barrier(jnp.sum(kernel, 1)), start_i)
            degree = add_at(degree, lax.optimization_barrier(jnp.sum(kernel, 0)) * mirror, start_j)
            return (image, degree)
        return (lax.cond(used_flag, apply_tile, keep_state, carried), None)
    initial = (jnp.zeros((RHS, POINTS), jnp.float32), jnp.zeros((POINTS,), jnp.float32))
    (coupled, degree), _ = lax.scan(one_tile, initial, (big_rows, big_cols, used_flags))
    image = (noise + degree)[None, :] * direction + coupled
    curvature = symmetric(gram(direction, image))
    norms_now = symmetric(gram(residual, residual))
    alpha = spd_solve(curvature, norms_now)
    solution_next = solution + apply_left(alpha, direction)
    residual_next = residual - apply_left(alpha, image)
    norms_next = symmetric(gram(residual_next, residual_next))
    beta = spd_solve(norms_now, norms_next)
    direction_next = residual_next + apply_left(beta, direction)
    return (solution_next, residual_next, direction_next)
```

```python
import functools
import math

import jax
import jax.numpy as jnp
from jax import lax
from jax.experimental import pallas as pl
from jax.experimental.pallas import tpu as pltpu
from jax.sharding import PartitionSpec as P

BLK_DEV = 4
DEPTH = 256
STACK = 48

HIGH = lax.Precision.HIGHEST
BF16 = jnp.bfloat16
F32 = jnp.float32

CUT = 0.25 ** 0.2
TOP = 5.0 * CUT**4
EDGE = 1.0 / CUT


def parts3(x):
    high = x.astype(BF16).astype(F32)
    rest = x - high
    mid = rest.astype(BF16).astype(F32)
    return high, mid, (rest - mid).astype(BF16).astype(F32)


def stack_features(x, left):
    width = x.shape[1]
    norm = jnp.sum(x * x, 0, keepdims=True)
    high, mid, low = parts3(x)
    n_high, n_mid, n_low = parts3(norm)
    ones = jnp.ones((1, width), F32)
    zero = jnp.zeros((2, width), F32)
    if left:
        rows = [high, high, mid, mid, high, low]
        rows += [jnp.concatenate([n_high, n_mid, n_low, ones, ones, ones, zero], 0)]
    else:
        high, mid, low = -2.0 * high, -2.0 * mid, -2.0 * low
        rows = [high, mid, high, mid, low, high]
        rows += [jnp.concatenate([ones, ones, ones, n_high, n_mid, n_low, zero], 0)]
    used = sum(r.shape[0] for r in rows)
    rows += [jnp.zeros((DEPTH - used, width), F32)]
    return jnp.concatenate(rows, 0)


def stack_directions(d):
    high = d.astype(BF16)
    low = (d - high.astype(F32)).astype(BF16)
    return jnp.concatenate([high, low, jnp.ones_like(high)], 0)


def dot(a, b, ca, cb):
    return lax.dot_general(a, b, (((ca,), (cb,)), ((), ())), preferred_element_type=F32)


def tiles_body(
    rows_ref, cols_ref, count_ref, rf_ref, rd_ref, cf_ref, cd_ref,
    to_row, to_col, left, right, d_row, d_col, acc_row, acc_col, *, chunk
):
    n_row, n_col = acc_row.shape[0], acc_col.shape[0]
    side = rd_ref.shape[0]
    width = acc_row.shape[2]
    scale = EDGE / (1.5 * math.sqrt(rf_ref.shape[0]))
    rank_row = lax.axis_index("row")
    rank_col = lax.axis_index("col")
    span = lax.axis_size("col") * BLK_DEV

    def prep_row(b, _):
        at = pl.ds(pl.multiple_of(b * width, width), width)
        left[b] = stack_features(rf_ref[:, at] * scale, True).T.astype(BF16)
        d_row[b] = stack_directions(rd_ref[:, at])
        acc_row[b] = jnp.zeros(acc_row.shape[1:], F32)
        return 0

    def prep_col(b, _):
        at = pl.ds(pl.multiple_of(b * width, width), width)
        right[b] = stack_features(cf_ref[:, at] * scale, False).astype(BF16)
        d_col[b] = stack_directions(cd_ref[:, at])
        acc_col[b] = jnp.zeros(acc_col.shape[1:], F32)
        return 0

    lax.fori_loop(0, n_row, prep_row, 0)
    lax.fori_loop(0, n_col, prep_col, 0)

    def one_tile(t, _):
        i = rows_ref[0, 0, t]
        j = cols_ref[0, 0, t]
        big_i = rank_row * span + i
        big_j = j // BLK_DEV * span + rank_col * BLK_DEV + j % BLK_DEV
        mirror = (big_i != big_j).astype(F32)
        points_j = right[j]
        dirs_j = d_col[j]
        into_col = None
        for c in range(width // chunk):
            at = slice(c * chunk, (c + 1) * chunk)
            dist = jnp.maximum(dot(left[i, at, :], points_j, 1, 0), 1e-30)
            v = jnp.maximum(EDGE - dist * lax.rsqrt(dist), 0.0)
            v2 = v * v
            kern = v2 * v2 * (TOP - v)
            k_high = kern.astype(BF16)
            k_low = (kern - k_high.astype(F32)).astype(BF16)
            acc_row[i, :, at] += dot(dirs_j, k_high, 1, 1) + dot(dirs_j, k_low, 1, 1)
            dirs_i = d_row[i, :, at]
            term = dot(dirs_i, k_high, 1, 0) + dot(dirs_i, k_low, 1, 0)
            into_col = term if into_col is None else into_col + term
        acc_col[j] += into_col * mirror
        return 0

    lax.fori_loop(0, count_ref[0, 0], one_tile, 0)

    def finish(acc, out):
        def one(b, _):
            whole = acc[b]
            out[b, :side] = whole[:side] + whole[side : 2 * side]
            out[b, side:] = whole[2 * side : 2 * side + 8]
            return 0

        lax.fori_loop(0, acc.shape[0], one, 0)

    finish(acc_row, to_row)
    finish(acc_col, to_col)


def tiles_call(rows, cols, count, rf, rd, cf, cd, width):
    n_row, n_col = rf.shape[1] // width, cf.shape[1] // width
    side = rd.shape[0]
    smem = pl.BlockSpec(memory_space=pltpu.SMEM)
    vmem = pl.BlockSpec(memory_space=pltpu.VMEM)
    return pl.pallas_call(
        functools.partial(tiles_body, chunk=256),
        out_shape=(
            jax.ShapeDtypeStruct((n_row, side + 8, width), F32),
            jax.ShapeDtypeStruct((n_col, side + 8, width), F32),
        ),
        in_specs=[smem] * 3 + [vmem] * 4,
        out_specs=(vmem, vmem),
        scratch_shapes=[
            pltpu.VMEM((n_row, width, DEPTH), BF16),
            pltpu.VMEM((n_col, DEPTH, width), BF16),
            pltpu.VMEM((n_row, STACK, width), BF16),
            pltpu.VMEM((n_col, STACK, width), BF16),
            pltpu.VMEM((n_row, STACK, width), F32),
            pltpu.VMEM((n_col, STACK, width), F32),
        ],
        compiler_params=pltpu.CompilerParams(vmem_limit_bytes=60 * 2**20),
        name="tiles",
    )(rows, cols, count, rf, rd, cf, cd)


def gram(left, right):
    return lax.dot_general(
        left, right, (((1,), (1,)), ((), ())), precision=HIGH, preferred_element_type=F32
    )


def symmetric(matrix):
    return 0.5 * (matrix + matrix.T)


def spd_solve(matrix, target):
    lower = jnp.linalg.cholesky(matrix)
    half_way = lax.linalg.triangular_solve(lower, target, left_side=True, lower=True)
    return lax.linalg.triangular_solve(
        lower, half_way, left_side=True, lower=True, transpose_a=True
    )


def apply_left(coeffs, field):
    return lax.dot_general(
        coeffs, field, (((0,), (0,)), ((), ())), precision=HIGH, preferred_element_type=F32
    )


def on_device(features, noise, solution, residual, direction, tile_rows, tile_cols, tile_count):
    width = features.shape[1] // BLK_DEV
    side = direction.shape[0]
    row_feat = lax.all_gather(features, "col", axis=1, tiled=True)
    row_dir = lax.all_gather(direction, "col", axis=1, tiled=True)
    col_feat = lax.all_gather(features, "row", axis=1, tiled=True)
    col_dir = lax.all_gather(direction, "row", axis=1, tiled=True)
    to_row, to_col = tiles_call(
        tile_rows, tile_cols, tile_count, row_feat, row_dir, col_feat, col_dir, width
    )
    mine = lax.psum_scatter(to_row, "col", scatter_dimension=0, tiled=True)
    mine = mine + lax.psum_scatter(to_col, "row", scatter_dimension=0, tiled=True)
    mine = jnp.transpose(mine, (1, 0, 2)).reshape(side + 8, BLK_DEV * width)
    image = (noise + mine[side])[None, :] * direction + mine[:side]
    curv_sum, norm_sum = lax.psum(
        (gram(direction, image), gram(residual, residual)), ("row", "col")
    )
    curvature = symmetric(curv_sum)
    norms_now = symmetric(norm_sum)
    alpha = spd_solve(curvature, norms_now)
    residual_next = residual - apply_left(alpha, image)
    norms_next = symmetric(lax.psum(gram(residual_next, residual_next), ("row", "col")))
    solution_next = solution + apply_left(alpha, direction)
    beta = spd_solve(norms_now, norms_next)
    direction_next = residual_next + apply_left(beta, direction)
    return (solution_next, residual_next, direction_next)


def solution(mesh):
    points = P(None, ("groups", "row", "col"))
    in_specs = (
        points,
        P(("groups", "row", "col")),
        points,
        points,
        points,
        P(("groups", "row"), "col", None),
        P(("groups", "row"), "col", None),
        P(("groups", "row"), "col"),
    )
    return jax.shard_map(
        on_device, mesh=mesh, in_specs=in_specs, out_specs=(points,) * 3, check_vma=False
    )
```

```python
import functools
import math

import jax
import jax.numpy as jnp
from jax import lax
from jax.experimental import pallas as pl
from jax.experimental.pallas import tpu as pltpu
from jax.sharding import PartitionSpec as P

BLK_DEV = 4
DEPTH = 256
STACK = 48

HIGH = lax.Precision.HIGHEST
BF16 = jnp.bfloat16
F32 = jnp.float32

CUT = 0.25 ** 0.2
TOP = 5.0 * CUT**4
EDGE = 1.0 / CUT


def parts3(x):
    high = x.astype(BF16).astype(F32)
    rest = x - high
    mid = rest.astype(BF16).astype(F32)
    return high, mid, (rest - mid).astype(BF16).astype(F32)


def stack_features(x, left):
    width = x.shape[1]
    norm = jnp.sum(x * x, 0, keepdims=True)
    high, mid, low = parts3(x)
    n_high, n_mid, n_low = parts3(norm)
    ones = jnp.ones((1, width), F32)
    zero = jnp.zeros((2, width), F32)
    if left:
        rows = [high, high, mid, mid, high, low]
        rows += [jnp.concatenate([n_high, n_mid, n_low, ones, ones, ones, zero], 0)]
    else:
        high, mid, low = -2.0 * high, -2.0 * mid, -2.0 * low
        rows = [high, mid, high, mid, low, high]
        rows += [jnp.concatenate([ones, ones, ones, n_high, n_mid, n_low, zero], 0)]
    used = sum(r.shape[0] for r in rows)
    rows += [jnp.zeros((DEPTH - used, width), F32)]
    return jnp.concatenate(rows, 0)


def stack_directions(d):
    high = d.astype(BF16)
    low = (d - high.astype(F32)).astype(BF16)
    return jnp.concatenate([high, low, jnp.ones_like(high)], 0)


def dot(a, b, ca, cb):
    return lax.dot_general(a, b, (((ca,), (cb,)), ((), ())), preferred_element_type=F32)


def tiles_body(
    rows_ref, cols_ref, count_ref, rf_ref, rd_ref, cf_ref, cd_ref,
    to_row, to_col, left, right, d_row, d_col, acc_row, acc_col, *, chunk
):
    n_row, n_col = acc_row.shape[0], acc_col.shape[0]
    side = rd_ref.shape[0]
    width = acc_row.shape[2]
    scale = EDGE / (1.5 * math.sqrt(rf_ref.shape[0]))
    rank_row = lax.axis_index("row")
    rank_col = lax.axis_index("col")
    span = lax.axis_size("col") * BLK_DEV

    def prep_row(b, _):
        at = pl.ds(pl.multiple_of(b * width, width), width)
        left[b] = stack_features(rf_ref[:, at] * scale, True).T.astype(BF16)
        d_row[b] = stack_directions(rd_ref[:, at])
        acc_row[b] = jnp.zeros(acc_row.shape[1:], F32)
        return 0

    def prep_col(b, _):
        at = pl.ds(pl.multiple_of(b * width, width), width)
        right[b] = stack_features(cf_ref[:, at] * scale, False).astype(BF16)
        d_col[b] = stack_directions(cd_ref[:, at])
        acc_col[b] = jnp.zeros(acc_col.shape[1:], F32)
        return 0

    lax.fori_loop(0, n_row, prep_row, 0)
    lax.fori_loop(0, n_col, prep_col, 0)

    def one_tile(t, _):
        i = rows_ref[0, 0, t]
        j = cols_ref[0, 0, t]
        big_i = rank_row * span + i
        big_j = j // BLK_DEV * span + rank_col * BLK_DEV + j % BLK_DEV
        mirror = (big_i != big_j).astype(F32)
        points_j = right[j]
        dirs_j = d_col[j]
        into_col = None
        for c in range(width // chunk):
            at = slice(c * chunk, (c + 1) * chunk)
            dist = jnp.maximum(dot(left[i, at, :], points_j, 1, 0), 1e-30)
            v = jnp.maximum(EDGE - dist * lax.rsqrt(dist), 0.0)
            v2 = v * v
            kern = v2 * v2 * (TOP - v)
            kern = kern.astype(BF16)
            acc_row[i, :, at] += dot(dirs_j, kern, 1, 1)
            term = dot(d_row[i, :, at], kern, 1, 0)
            into_col = term if into_col is None else into_col + term
        acc_col[j] += into_col * mirror
        return 0

    lax.fori_loop(0, count_ref[0, 0], one_tile, 0)

    def finish(acc, out):
        def one(owner, _):
            degrees = []
            for b in range(BLK_DEV):
                whole = acc[owner * BLK_DEV + b]
                out[owner, b * side : (b + 1) * side] = whole[:side] + whole[side : 2 * side]
                degrees.append(whole[2 * side : 2 * side + 1])
            degrees.append(jnp.zeros((8 - BLK_DEV, width), F32))
            out[owner, BLK_DEV * side :] = jnp.concatenate(degrees, 0)
            return 0

        lax.fori_loop(0, acc.shape[0] // BLK_DEV, one, 0)

    finish(acc_row, to_row)
    finish(acc_col, to_col)


def tiles_call(rows, cols, count, rf, rd, cf, cd, width):
    n_row, n_col = rf.shape[1] // width, cf.shape[1] // width
    side = rd.shape[0]
    smem = pl.BlockSpec(memory_space=pltpu.SMEM)
    vmem = pl.BlockSpec(memory_space=pltpu.VMEM)
    return pl.pallas_call(
        functools.partial(tiles_body, chunk=512),
        out_shape=(
            jax.ShapeDtypeStruct((n_row // BLK_DEV, BLK_DEV * side + 8, width), F32),
            jax.ShapeDtypeStruct((n_col // BLK_DEV, BLK_DEV * side + 8, width), F32),
        ),
        in_specs=[smem] * 3 + [vmem] * 4,
        out_specs=(vmem, vmem),
        scratch_shapes=[
            pltpu.VMEM((n_row, width, DEPTH), BF16),
            pltpu.VMEM((n_col, DEPTH, width), BF16),
            pltpu.VMEM((n_row, STACK, width), BF16),
            pltpu.VMEM((n_col, STACK, width), BF16),
            pltpu.VMEM((n_row, STACK, width), F32),
            pltpu.VMEM((n_col, STACK, width), F32),
        ],
        compiler_params=pltpu.CompilerParams(vmem_limit_bytes=60 * 2**20),
        name="tiles",
    )(rows, cols, count, rf, rd, cf, cd)


def exact_dot(a, b, ca, cb):
    return lax.dot_general(
        a, b, (((ca,), (cb,)), ((), ())), precision=HIGH, preferred_element_type=F32
    )


def invert(matrix):
    n = matrix.shape[0]
    rows = lax.broadcasted_iota(jnp.int32, (n, n), 0)
    cols = lax.broadcasted_iota(jnp.int32, (n, n), 1)
    both = jnp.concatenate([matrix, (rows == cols).astype(F32)], 1)
    at = lax.broadcasted_iota(jnp.int32, both.shape, 0)
    for k in range(n):
        pivot_row = both[k : k + 1, :] / both[k : k + 1, k : k + 1]
        both = jnp.where(at == k, pivot_row, both - both[:, k : k + 1] * pivot_row)
    return both[:, n:]


MESH = pl.DeviceIdType.MESH


def exchange(name, n, source, landing, send_sem, recv_sem):
    me = lax.axis_index(name)
    copies = []
    for d in range(1, n):
        owner = lax.rem(me + d, n)
        copies.append(
            pltpu.make_async_remote_copy(
                src_ref=source(owner),
                dst_ref=landing.at[d - 1],
                send_sem=send_sem.at[d - 1],
                recv_sem=recv_sem.at[d - 1],
                device_id={name: owner},
                device_id_type=MESH,
            )
        )
        copies[-1].start()
    return copies


def greet(sizes):
    barrier = pltpu.get_barrier_semaphore()
    total = 0
    for name, n in sizes:
        me = lax.axis_index(name)
        for d in range(1, n):
            pl.semaphore_signal(
                barrier, inc=1, device_id={name: lax.rem(me + d, n)}, device_id_type=MESH
            )
        total += n - 1
    pl.semaphore_wait(barrier, total)


def tail_body(
    to_row, to_col, noise, sol, res, direction, sol_out, res_out, dir_out,
    land_row, land_col, image, own, land_a, land_b,
    s_row, r_row, s_col, r_col, s_a, r_a, s_b, r_b, *, n_row, n_col
):
    side = direction.shape[0]
    width = to_row.shape[2]
    greet((("row", n_row), ("col", n_col)))
    over_col = exchange("col", n_col, lambda o: to_row.at[o], land_row, s_row, r_row)
    over_row = exchange("row", n_row, lambda o: to_col.at[o], land_col, s_col, r_col)
    d = direction[...]
    r = res[...]
    gram_res = exact_dot(r, r, 1, 1)
    for copy in over_row:
        copy.wait_recv()
    for copy in over_col:
        copy.wait_recv()
    total = to_row[lax.axis_index("col")] + to_col[lax.axis_index("row")]
    for k in range(n_col - 1):
        total += land_row[k]
    for k in range(n_row - 1):
        total += land_col[k]
    for b in range(BLK_DEV):
        at = slice(b * width, (b + 1) * width)
        shift = noise[:, at] + total[BLK_DEV * side + b : BLK_DEV * side + b + 1]
        image[:, at] = shift * d[:, at] + total[b * side : (b + 1) * side]
    im = image[...]

    def all_sum(turn, value):
        for stage, (name, n, landing, send, recv) in enumerate(
            (("row", n_row, land_a, s_a, r_a), ("col", n_col, land_b, s_b, r_b))
        ):
            mine = own.at[2 * turn + stage]
            mine[...] = value
            copies = exchange(
                name, n, lambda o: mine, landing.at[turn], send.at[turn], recv.at[turn]
            )
            for k, copy in enumerate(copies):
                copy.wait_recv()
            for k in range(n - 1):
                value = value + landing[turn, k]
            waiting.extend(copies)
        return value

    waiting = over_row + over_col
    curv = 0.5 * (exact_dot(d, im, 1, 1) + exact_dot(im, d, 1, 1))
    blank = jnp.zeros((side, 128 - 2 * side), F32)
    sums = all_sum(0, jnp.concatenate([curv, gram_res, blank], 1))
    norms = sums[:, side : 2 * side]
    curv_inv = invert(sums[:, :side])
    norms_inv = invert(norms)
    alpha_t = exact_dot(norms, curv_inv, 1, 0)
    r_next = r - exact_dot(alpha_t, im, 1, 0)
    res_out[...] = r_next
    gram_next = exact_dot(r_next, r_next, 1, 1)
    blank = jnp.zeros((side, 128 - side), F32)
    sol_out[...] = sol[...] + exact_dot(alpha_t, d, 1, 0)
    norms_next = all_sum(1, jnp.concatenate([gram_next, blank], 1))[:, :side]
    beta_t = exact_dot(norms_next, norms_inv, 1, 0)
    dir_out[...] = r_next + exact_dot(beta_t, d, 1, 0)
    for copy in waiting:
        copy.wait_send()


def tail_call(to_row, to_col, noise, sol, res, direction):
    n_col, n_row = to_row.shape[0], to_col.shape[0]
    side, points = direction.shape
    vmem = pl.BlockSpec(memory_space=pltpu.VMEM)
    shape = jax.ShapeDtypeStruct((side, points), F32)
    dma = pltpu.SemaphoreType.DMA
    return pl.pallas_call(
        functools.partial(tail_body, n_row=n_row, n_col=n_col),
        out_shape=(shape,) * 3,
        in_specs=[vmem] * 6,
        out_specs=(vmem,) * 3,
        scratch_shapes=[
            pltpu.VMEM((n_col - 1,) + to_row.shape[1:], F32),
            pltpu.VMEM((n_row - 1,) + to_col.shape[1:], F32),
            pltpu.VMEM((side, points), F32),
            pltpu.VMEM((4, side, 128), F32),
            pltpu.VMEM((2, n_row - 1, side, 128), F32),
            pltpu.VMEM((2, n_col - 1, side, 128), F32),
            dma((n_col - 1,)), dma((n_col - 1,)),
            dma((n_row - 1,)), dma((n_row - 1,)),
            dma((2, n_row - 1)), dma((2, n_row - 1)),
            dma((2, n_col - 1)), dma((2, n_col - 1)),
        ],
        compiler_params=pltpu.CompilerParams(
            collective_id=1, has_side_effects=True, vmem_limit_bytes=40 * 2**20
        ),
        name="tail",
    )(to_row, to_col, noise, sol, res, direction)


def on_device(features, noise, solution, residual, direction, tile_rows, tile_cols, tile_count):
    width = features.shape[1] // BLK_DEV
    side = direction.shape[0]
    row_feat = lax.all_gather(features, "col", axis=1, tiled=True)
    row_dir = lax.all_gather(direction, "col", axis=1, tiled=True)
    col_feat = lax.all_gather(features, "row", axis=1, tiled=True)
    col_dir = lax.all_gather(direction, "row", axis=1, tiled=True)
    to_row, to_col = tiles_call(
        tile_rows, tile_cols, tile_count, row_feat, row_dir, col_feat, col_dir, width
    )
    return tail_call(to_row, to_col, noise[None, :], solution, residual, direction)


def solution(mesh):
    points = P(None, ("groups", "row", "col"))
    in_specs = (
        points,
        P(("groups", "row", "col")),
        points,
        points,
        points,
        P(("groups", "row"), "col", None),
        P(("groups", "row"), "col", None),
        P(("groups", "row"), "col"),
    )
    return jax.shard_map(
        on_device, mesh=mesh, in_specs=in_specs, out_specs=(points,) * 3, check_vma=False
    )
```

```python
import functools
import math

import jax
import jax.numpy as jnp
from jax import lax
from jax.experimental import pallas as pl
from jax.experimental.pallas import tpu as pltpu
from jax.sharding import PartitionSpec as P

BLK_DEV = 4
DEPTH = 208
STACK = 48

HIGH = lax.Precision.HIGHEST
BF16 = jnp.bfloat16
F32 = jnp.float32

CUT = 0.25 ** 0.2
TOP = 5.0 * CUT**4
EDGE = 1.0 / CUT


def parts3(x):
    high = x.astype(BF16).astype(F32)
    rest = x - high
    mid = rest.astype(BF16).astype(F32)
    return high, mid, (rest - mid).astype(BF16).astype(F32)


def stack_features(x, left):
    width = x.shape[1]
    norm = jnp.sum(x * x, 0, keepdims=True)
    high, mid, low = parts3(x)
    n_high, n_mid, n_low = parts3(norm)
    ones = jnp.ones((1, width), F32)
    zero = jnp.zeros((2, width), F32)
    if left:
        rows = [high, high, mid, mid, high, low]
        rows += [jnp.concatenate([n_high, n_mid, n_low, ones, ones, ones, zero], 0)]
    else:
        high, mid, low = -2.0 * high, -2.0 * mid, -2.0 * low
        rows = [high, mid, high, mid, low, high]
        rows += [jnp.concatenate([ones, ones, ones, n_high, n_mid, n_low, zero], 0)]
    used = sum(r.shape[0] for r in rows)
    rows += [jnp.zeros((DEPTH - used, width), F32)]
    return jnp.concatenate(rows, 0)


def stack_directions(d):
    high = d.astype(BF16)
    low = (d - high.astype(F32)).astype(BF16)
    return jnp.concatenate([high, low, jnp.ones_like(high)], 0)


def dot(a, b, ca, cb):
    return lax.dot_general(a, b, (((ca,), (cb,)), ((), ())), preferred_element_type=F32)


def prep_body(rows_ref, cols_ref, count_ref, *refs, n_row, n_col):
    pieces, (right, d_col, slots, totals) = refs[:n_row], refs[n_row:]
    width = right.shape[2]
    feat = pieces[0].shape[0] - d_col.shape[1] // 3
    scale = EDGE / (1.5 * math.sqrt(feat))
    me = lax.axis_index("row")
    col = lax.axis_index("col")
    for p in range(n_col):
        totals[p] = 0

    def sort(t, _):
        i, j = rows_ref[0, 0, t], cols_ref[0, 0, t]
        p = lax.rem(col - i // BLK_DEV + n_col, n_col)
        at = totals[p]
        slots[p, at] = i * (n_row * BLK_DEV) + j
        totals[p] = at + 1
        return 0

    lax.fori_loop(0, count_ref[0, 0], sort, 0)
    for k, piece in enumerate(pieces):
        core = lax.rem(me, 2) if k < n_row // 2 else 1 - lax.rem(me, 2)
        place = lax.rem(me // 2 - k % (n_row // 2) + n_row // 2, n_row // 2)
        first = (2 * place + core) * BLK_DEV
        for b in range(BLK_DEV):
            at = slice(b * width, (b + 1) * width)
            right[first + b] = stack_features(piece[:feat, at] * scale, False).astype(BF16)
            d_col[first + b] = stack_directions(piece[feat:, at])


def prep_call(rows, cols, count, pieces, side, n_col):
    n_row = len(pieces)
    width = pieces[0].shape[1] // BLK_DEV
    smem = pl.BlockSpec(memory_space=pltpu.SMEM)
    vmem = pl.BlockSpec(memory_space=pltpu.VMEM)
    return pl.pallas_call(
        functools.partial(prep_body, n_row=n_row, n_col=n_col),
        out_shape=(
            jax.ShapeDtypeStruct((n_row * BLK_DEV, DEPTH, width), BF16),
            jax.ShapeDtypeStruct((n_row * BLK_DEV, 3 * side, width), BF16),
            jax.ShapeDtypeStruct((n_col, rows.shape[2]), jnp.int32),
            jax.ShapeDtypeStruct((n_col,), jnp.int32),
        ),
        in_specs=[smem] * 3 + [vmem] * n_row,
        out_specs=(vmem, vmem, smem, smem),
        compiler_params=pltpu.CompilerParams(vmem_limit_bytes=40 * 2**20),
        cost_estimate=pl.CostEstimate(
            flops=2 * 10**9, bytes_accessed=8 * 2**20, transcendentals=0
        ),
        name="prep",
    )(rows, cols, count, *pieces)


def phase_body(slots, totals, piece, right, d_col, *refs, phase, n_row, n_col):
    first, last = phase == 0, phase == n_col - 1
    acc_in = None if first else refs[0]
    to_row, to_col, left, d_row, acc_row = refs[0 if first else 1 :][:5]
    acc_col = refs[-1] if last else to_col
    width = right.shape[2]
    side = d_col.shape[1] // 3
    feat = piece.shape[0] - side
    scale = EDGE / (1.5 * math.sqrt(feat))
    n_blocks = n_row * BLK_DEV
    rank_row = lax.axis_index("row")
    rank_col = lax.axis_index("col")
    owner = lax.rem(rank_col - phase + n_col, n_col)
    span = n_col * BLK_DEV
    for b in range(BLK_DEV):
        at = slice(b * width, (b + 1) * width)
        left[b] = stack_features(piece[:feat, at] * scale, True).T.astype(BF16)
        d_row[b] = stack_directions(piece[feat:, at])
    acc_row[...] = jnp.zeros_like(acc_row)

    def carry_over(b, _):
        acc_col[b] = jnp.zeros(acc_col.shape[1:], F32) if first else acc_in[b]
        return 0

    lax.fori_loop(0, n_blocks, carry_over, 0)

    def one_tile(t, _):
        pair = slots[phase, t]
        j = lax.rem(pair, n_blocks)
        i = pair // n_blocks
        big_i = rank_row * span + i
        big_j = j // BLK_DEV * span + rank_col * BLK_DEV + j % BLK_DEV
        mirror = (big_i != big_j).astype(F32)
        i = i - owner * BLK_DEV
        dist = jnp.maximum(dot(left[i], right[j], 1, 0), 1e-30)
        v = jnp.maximum(EDGE - dist * lax.rsqrt(dist), 0.0)
        v2 = v * v
        kern = (v2 * v2 * (TOP - v)).astype(BF16)
        acc_row[i] += dot(d_col[j], kern, 1, 1)
        acc_col[j] += dot(d_row[i], kern, 1, 0) * mirror
        return 0

    lax.fori_loop(0, totals[phase], one_tile, 0)

    def finish(acc, owner_at, out):
        degrees = []
        for b in range(BLK_DEV):
            whole = acc[owner_at * BLK_DEV + b]
            out[b * side : (b + 1) * side] = whole[:side] + whole[side : 2 * side]
            degrees.append(whole[2 * side : 2 * side + 1])
        degrees.append(jnp.zeros((8 - BLK_DEV, width), F32))
        out[BLK_DEV * side :] = jnp.concatenate(degrees, 0)

    finish(acc_row, 0, to_row)
    if last:

        def one(o, _):
            finish(acc_col, o, to_col.at[o])
            return 0

        lax.fori_loop(0, n_row, one, 0)


def phase_call(slots, totals, piece, right, d_col, acc, phase, n_row, n_col):
    width = right.shape[2]
    stack = d_col.shape[1]
    side = stack // 3
    first, last = phase == 0, phase == n_col - 1
    smem = pl.BlockSpec(memory_space=pltpu.SMEM)
    vmem = pl.BlockSpec(memory_space=pltpu.VMEM)
    packed = (BLK_DEV * side + 8, width)
    sums = (n_row * BLK_DEV, stack, width)
    scratch = [
        pltpu.VMEM((BLK_DEV, width, DEPTH), BF16),
        pltpu.VMEM((BLK_DEV, stack, width), BF16),
        pltpu.VMEM((BLK_DEV, stack, width), F32),
    ]
    if last:
        scratch.append(pltpu.VMEM(sums, F32))
    accs = () if first else (acc,)
    return pl.pallas_call(
        functools.partial(phase_body, phase=phase, n_row=n_row, n_col=n_col),
        out_shape=(
            jax.ShapeDtypeStruct(packed, F32),
            jax.ShapeDtypeStruct((n_row,) + packed if last else sums, F32),
        ),
        in_specs=[smem] * 2 + [vmem] * (3 + len(accs)),
        out_specs=(vmem, vmem),
        scratch_shapes=scratch,
        compiler_params=pltpu.CompilerParams(vmem_limit_bytes=36 * 2**20),
        cost_estimate=pl.CostEstimate(
            flops=14 * 10**9, bytes_accessed=8 * 2**20, transcendentals=0
        ),
        name=f"phase{phase}",
    )(slots, totals, piece, right, d_col, *accs)


def exact_dot(a, b, ca, cb):
    return lax.dot_general(
        a, b, (((ca,), (cb,)), ((), ())), precision=HIGH, preferred_element_type=F32
    )


def invert(matrix):
    n = matrix.shape[0]
    rows = lax.broadcasted_iota(jnp.int32, (n, n), 0)
    cols = lax.broadcasted_iota(jnp.int32, (n, n), 1)
    both = jnp.concatenate([matrix, (rows == cols).astype(F32)], 1)
    at = lax.broadcasted_iota(jnp.int32, both.shape, 0)
    for k in range(n):
        pivot_row = both[k : k + 1, :] / both[k : k + 1, k : k + 1]
        both = jnp.where(at == k, pivot_row, both - both[:, k : k + 1] * pivot_row)
    return both[:, n:]


MESH = pl.DeviceIdType.MESH


def exchange(name, n, source, landing, send_sem, recv_sem, stop=None):
    me = lax.axis_index(name)
    copies = []
    for d in range(1, stop or n):
        owner = lax.rem(me + d, n)
        copies.append(
            pltpu.make_async_remote_copy(
                src_ref=source(owner),
                dst_ref=landing.at[d - 1],
                send_sem=send_sem.at[d - 1],
                recv_sem=recv_sem.at[d - 1],
                device_id={name: owner},
                device_id_type=MESH,
            )
        )
        copies[-1].start()
    return copies


def greet(sizes):
    barrier = pltpu.get_barrier_semaphore()
    total = 0
    for name, n in sizes:
        me = lax.axis_index(name)
        for d in range(1, n):
            pl.semaphore_signal(
                barrier, inc=1, device_id={name: lax.rem(me + d, n)}, device_id_type=MESH
            )
        total += n - 1
    pl.semaphore_wait(barrier, total)


def tail_body(*refs, n_row, n_col):
    homed = refs[: n_col - 1]
    (
        to_row, to_col, noise, sol, res, direction, sol_out, res_out, dir_out,
        land_row, land_col, image, own, land_a, land_b,
        s_row, r_row, s_col, r_col, s_a, r_a, s_b, r_b,
    ) = refs[n_col - 1 :]
    side = direction.shape[0]
    width = to_row.shape[1]
    greet((("row", n_row), ("col", n_col)))
    over_col = exchange("col", n_col, lambda o: to_row, land_row, s_row, r_row, 2)
    over_row = exchange("row", n_row, lambda o: to_col.at[o], land_col, s_col, r_col)
    d = direction[...]
    r = res[...]
    gram_res = exact_dot(r, r, 1, 1)
    for copy in over_row:
        copy.wait_recv()
    for copy in over_col:
        copy.wait_recv()
    total = to_col[lax.axis_index("row")] + land_row[0]
    for part in homed:
        total += part[...]
    for k in range(n_row - 1):
        total += land_col[k]
    for b in range(BLK_DEV):
        at = slice(b * width, (b + 1) * width)
        shift = noise[:, at] + total[BLK_DEV * side + b : BLK_DEV * side + b + 1]
        image[:, at] = shift * d[:, at] + total[b * side : (b + 1) * side]
    im = image[...]

    def all_sum(turn, value):
        for stage, (name, n, landing, send, recv) in enumerate(
            (("row", n_row, land_a, s_a, r_a), ("col", n_col, land_b, s_b, r_b))
        ):
            mine = own.at[2 * turn + stage]
            mine[...] = value
            copies = exchange(
                name, n, lambda o: mine, landing.at[turn], send.at[turn], recv.at[turn]
            )
            for k, copy in enumerate(copies):
                copy.wait_recv()
            for k in range(n - 1):
                value = value + landing[turn, k]
            waiting.extend(copies)
        return value

    waiting = over_row + over_col
    curv = 0.5 * (exact_dot(d, im, 1, 1) + exact_dot(im, d, 1, 1))
    blank = jnp.zeros((side, 128 - 2 * side), F32)
    sums = all_sum(0, jnp.concatenate([curv, gram_res, blank], 1))
    norms = sums[:, side : 2 * side]
    curv_inv = invert(sums[:, :side])
    norms_inv = invert(norms)
    alpha_t = exact_dot(norms, curv_inv, 1, 0)
    r_next = r - exact_dot(alpha_t, im, 1, 0)
    res_out[...] = r_next
    gram_next = exact_dot(r_next, r_next, 1, 1)
    blank = jnp.zeros((side, 128 - side), F32)
    sol_out[...] = sol[...] + exact_dot(alpha_t, d, 1, 0)
    norms_next = all_sum(1, jnp.concatenate([gram_next, blank], 1))[:, :side]
    beta_t = exact_dot(norms_next, norms_inv, 1, 0)
    dir_out[...] = r_next + exact_dot(beta_t, d, 1, 0)
    for copy in waiting:
        copy.wait_send()


def tail_call(homed, to_row, to_col, noise, sol, res, direction):
    n_col, n_row = len(homed) + 1, to_col.shape[0]
    side, points = direction.shape
    vmem = pl.BlockSpec(memory_space=pltpu.VMEM)
    shape = jax.ShapeDtypeStruct((side, points), F32)
    dma = pltpu.SemaphoreType.DMA
    return pl.pallas_call(
        functools.partial(tail_body, n_row=n_row, n_col=n_col),
        out_shape=(shape,) * 3,
        in_specs=[vmem] * (6 + len(homed)),
        out_specs=(vmem,) * 3,
        scratch_shapes=[
            pltpu.VMEM((1,) + to_row.shape, F32),
            pltpu.VMEM((n_row - 1,) + to_col.shape[1:], F32),
            pltpu.VMEM((side, points), F32),
            pltpu.VMEM((4, side, 128), F32),
            pltpu.VMEM((2, n_row - 1, side, 128), F32),
            pltpu.VMEM((2, n_col - 1, side, 128), F32),
            dma((1,)), dma((1,)),
            dma((n_row - 1,)), dma((n_row - 1,)),
            dma((2, n_row - 1)), dma((2, n_row - 1)),
            dma((2, n_col - 1)), dma((2, n_col - 1)),
        ],
        compiler_params=pltpu.CompilerParams(
            collective_id=1, has_side_effects=True, vmem_limit_bytes=40 * 2**20
        ),
        name="tail",
    )(*homed, to_row, to_col, noise, sol, res, direction)


def on_device(features, noise, solution, residual, direction, tile_rows, tile_cols, tile_count):
    side = direction.shape[0]
    n_row, n_col = lax.axis_size("row"), lax.axis_size("col")
    own = jnp.concatenate([features, direction], 0)
    chips = n_row // 2

    def along_x(value):
        return lax.ppermute(value, "row", [(r, (r + 2) % n_row) for r in range(n_row)])

    def between_cores(value):
        return lax.ppermute(value, "row", [(r, r ^ 1) for r in range(n_row)])

    def along_col(value, step):
        return lax.ppermute(value, "col", [(c, (c + step) % n_col) for c in range(n_col)])

    ring = [own]
    for _ in range(n_col - 1):
        ring.append(along_col(ring[-1], 1))
    pieces = [own]
    for _ in range(chips - 1):
        pieces.append(along_x(pieces[-1]))
    pieces += [between_cores(piece) for piece in pieces]
    right, d_col, slots, totals = prep_call(
        tile_rows, tile_cols, tile_count, pieces, side, n_col
    )
    acc = None
    homed = []
    for p in range(n_col):
        to_row, acc = phase_call(slots, totals, ring[p], right, d_col, acc, p, n_row, n_col)
        if p < n_col - 1:
            homed.append(along_col(to_row, -p) if p else to_row)
    return tail_call(homed, to_row, acc, noise[None, :], solution, residual, direction)


def solution(mesh):
    points = P(None, ("groups", "row", "col"))
    in_specs = (
        points,
        P(("groups", "row", "col")),
        points,
        points,
        points,
        P(("groups", "row"), "col", None),
        P(("groups", "row"), "col", None),
        P(("groups", "row"), "col"),
    )
    return jax.shard_map(
        on_device, mesh=mesh, in_specs=in_specs, out_specs=(points,) * 3, check_vma=False
    )
```

```python
import functools
import math

import jax
import jax.numpy as jnp
from jax import lax
from jax.experimental import pallas as pl
from jax.experimental.pallas import tpu as pltpu
from jax.sharding import PartitionSpec as P

BLK_DEV = 4
DEPTH = 208
STACK = 48

HIGH = lax.Precision.HIGHEST
BF16 = jnp.bfloat16
F32 = jnp.float32

CUT = 0.25 ** 0.2
TOP = 5.0 * CUT**4
EDGE = 1.0 / CUT


def parts3(x):
    high = x.astype(BF16).astype(F32)
    rest = x - high
    mid = rest.astype(BF16).astype(F32)
    return high, mid, (rest - mid).astype(BF16).astype(F32)


def stack_features(x, left):
    width = x.shape[1]
    norm = jnp.sum(x * x, 0, keepdims=True)
    high, mid, low = parts3(x)
    n_high, n_mid, n_low = parts3(norm)
    ones = jnp.ones((1, width), F32)
    zero = jnp.zeros((2, width), F32)
    if left:
        rows = [high, high, mid, mid, high, low]
        rows += [jnp.concatenate([n_high, n_mid, n_low, ones, ones, ones, zero], 0)]
    else:
        high, mid, low = -2.0 * high, -2.0 * mid, -2.0 * low
        rows = [high, mid, high, mid, low, high]
        rows += [jnp.concatenate([ones, ones, ones, n_high, n_mid, n_low, zero], 0)]
    used = sum(r.shape[0] for r in rows)
    rows += [jnp.zeros((DEPTH - used, width), F32)]
    return jnp.concatenate(rows, 0)


def stack_directions(d):
    high = d.astype(BF16)
    low = (d - high.astype(F32)).astype(BF16)
    return jnp.concatenate([high, low, jnp.ones_like(high)], 0)


def dot(a, b, ca, cb):
    return lax.dot_general(a, b, (((ca,), (cb,)), ((), ())), preferred_element_type=F32)


def prep_body(pairs_ref, count_ref, *refs, n_row, n_col):
    pieces, (right, d_col, slots, totals) = refs[:n_row], refs[n_row:]
    width = right.shape[2]
    feat = pieces[0].shape[0] - d_col.shape[1] // 3
    scale = EDGE / (1.5 * math.sqrt(feat))
    me = lax.axis_index("row")
    col = lax.axis_index("col")
    for p in range(n_col):
        totals[p] = 0

    def sort(t, _):
        pair = pairs_ref[0, t]
        p = lax.rem(col - pair // (n_row * BLK_DEV * BLK_DEV) + n_col, n_col)
        at = totals[p]
        slots[p, at] = pair
        totals[p] = at + 1
        return 0

    lax.fori_loop(0, count_ref[0, 0], sort, 0)
    for k, piece in enumerate(pieces):
        core = lax.rem(me, 2) if k < n_row // 2 else 1 - lax.rem(me, 2)
        place = lax.rem(me // 2 - k % (n_row // 2) + n_row // 2, n_row // 2)
        first = (2 * place + core) * BLK_DEV
        for b in range(BLK_DEV):
            at = slice(b * width, (b + 1) * width)
            right[first + b] = stack_features(piece[:feat, at] * scale, False).astype(BF16)
            d_col[first + b] = stack_directions(piece[feat:, at])


def prep_call(pairs, count, pieces, side, n_col):
    n_row = len(pieces)
    width = pieces[0].shape[1] // BLK_DEV
    smem = pl.BlockSpec(memory_space=pltpu.SMEM)
    vmem = pl.BlockSpec(memory_space=pltpu.VMEM)
    return pl.pallas_call(
        functools.partial(prep_body, n_row=n_row, n_col=n_col),
        out_shape=(
            jax.ShapeDtypeStruct((n_row * BLK_DEV, DEPTH, width), BF16),
            jax.ShapeDtypeStruct((n_row * BLK_DEV, 3 * side, width), BF16),
            jax.ShapeDtypeStruct((n_col, pairs.shape[1]), jnp.int32),
            jax.ShapeDtypeStruct((n_col,), jnp.int32),
        ),
        in_specs=[smem] * 2 + [vmem] * n_row,
        out_specs=(vmem, vmem, smem, smem),
        compiler_params=pltpu.CompilerParams(vmem_limit_bytes=40 * 2**20),
        cost_estimate=pl.CostEstimate(
            flops=2 * 10**9, bytes_accessed=8 * 2**20, transcendentals=0
        ),
        name="prep",
    )(pairs, count, *pieces)


def phase_body(slots, totals, piece, right, d_col, *refs, phase, n_row, n_col):
    first, last = phase == 0, phase == n_col - 1
    acc_in = None if first else refs[0]
    to_row, to_col, left, d_row, acc_row, held_a, held_b = refs[0 if first else 1 :][:7]
    acc_col = refs[-1] if last else to_col
    width = right.shape[2]
    side = d_col.shape[1] // 3
    feat = piece.shape[0] - side
    scale = EDGE / (1.5 * math.sqrt(feat))
    n_blocks = n_row * BLK_DEV
    rank_row = lax.axis_index("row")
    rank_col = lax.axis_index("col")
    owner = lax.rem(rank_col - phase + n_col, n_col)
    span = n_col * BLK_DEV
    for b in range(BLK_DEV):
        at = slice(b * width, (b + 1) * width)
        left[b] = stack_features(piece[:feat, at] * scale, True).T.astype(BF16)
        d_row[b] = stack_directions(piece[feat:, at])
    acc_row[...] = jnp.zeros_like(acc_row)

    def carry_over(b, _):
        acc_col[b] = jnp.zeros(acc_col.shape[1:], F32) if first else acc_in[b]
        return 0

    lax.fori_loop(0, n_blocks, carry_over, 0)

    count = totals[phase]

    def place(t):
        pair = slots[phase, t]
        i = pair // n_blocks
        return i, lax.rem(pair, n_blocks)

    def evaluate(t, held):
        i, j = place(t)
        dist = jnp.maximum(dot(left[i - owner * BLK_DEV], right[j], 1, 0), 1e-30)
        v = jnp.maximum(EDGE - dist * lax.rsqrt(dist), 0.0)
        v2 = v * v
        held[...] = (v2 * v2 * (TOP - v)).astype(BF16)

    def multiply(t, held, used):
        i, j = place(t)
        big_i = rank_row * span + i
        big_j = j // BLK_DEV * span + rank_col * BLK_DEV + j % BLK_DEV
        mirror = (big_i != big_j).astype(F32) * used
        i = i - owner * BLK_DEV
        kern = held[...]
        into_row = dot(d_col[j], kern, 1, 1) * used
        into_col = dot(d_row[i], kern, 1, 0) * mirror
        acc_row[i] += into_row
        acc_col[j] += into_col

    def two_tiles(pair_at, _):
        t = 2 * pair_at
        second = jnp.minimum(t + 1, count - 1)
        evaluate(second, held_b)
        multiply(t, held_a, 1.0)
        evaluate(jnp.minimum(t + 2, count - 1), held_a)
        multiply(second, held_b, (t + 1 < count).astype(F32))
        return 0

    @pl.when(count > 0)
    def _():
        evaluate(0, held_a)
        lax.fori_loop(0, (count + 1) // 2, two_tiles, 0)

    def finish(acc, owner_at, out):
        degrees = []
        for b in range(BLK_DEV):
            whole = acc[owner_at * BLK_DEV + b]
            out[b * side : (b + 1) * side] = whole[:side] + whole[side : 2 * side]
            degrees.append(whole[2 * side : 2 * side + 1])
        degrees.append(jnp.zeros((8 - BLK_DEV, width), F32))
        out[BLK_DEV * side :] = jnp.concatenate(degrees, 0)

    finish(acc_row, 0, to_row)
    if last:

        def one(o, _):
            finish(acc_col, o, to_col.at[o])
            return 0

        lax.fori_loop(0, n_row, one, 0)


def phase_call(slots, totals, piece, right, d_col, acc, phase, n_row, n_col):
    width = right.shape[2]
    stack = d_col.shape[1]
    side = stack // 3
    first, last = phase == 0, phase == n_col - 1
    smem = pl.BlockSpec(memory_space=pltpu.SMEM)
    vmem = pl.BlockSpec(memory_space=pltpu.VMEM)
    packed = (BLK_DEV * side + 8, width)
    sums = (n_row * BLK_DEV, stack, width)
    scratch = [
        pltpu.VMEM((BLK_DEV, width, DEPTH), BF16),
        pltpu.VMEM((BLK_DEV, stack, width), BF16),
        pltpu.VMEM((BLK_DEV, stack, width), F32),
        pltpu.VMEM((width, width), BF16),
        pltpu.VMEM((width, width), BF16),
    ]
    if last:
        scratch.append(pltpu.VMEM(sums, F32))
    accs = () if first else (acc,)
    return pl.pallas_call(
        functools.partial(phase_body, phase=phase, n_row=n_row, n_col=n_col),
        out_shape=(
            jax.ShapeDtypeStruct(packed, F32),
            jax.ShapeDtypeStruct((n_row,) + packed if last else sums, F32),
        ),
        in_specs=[smem] * 2 + [vmem] * (3 + len(accs)),
        out_specs=(vmem, vmem),
        scratch_shapes=scratch,
        compiler_params=pltpu.CompilerParams(vmem_limit_bytes=36 * 2**20),
        cost_estimate=pl.CostEstimate(
            flops=14 * 10**9, bytes_accessed=8 * 2**20, transcendentals=0
        ),
        name=f"phase{phase}",
    )(slots, totals, piece, right, d_col, *accs)


def exact_dot(a, b, ca, cb):
    return lax.dot_general(
        a, b, (((ca,), (cb,)), ((), ())), precision=HIGH, preferred_element_type=F32
    )


def invert(matrix):
    n = matrix.shape[0]
    rows = lax.broadcasted_iota(jnp.int32, (n, n), 0)
    cols = lax.broadcasted_iota(jnp.int32, (n, n), 1)
    both = jnp.concatenate([matrix, (rows == cols).astype(F32)], 1)
    at = lax.broadcasted_iota(jnp.int32, both.shape, 0)
    for k in range(n):
        pivot_row = both[k : k + 1, :] / both[k : k + 1, k : k + 1]
        both = jnp.where(at == k, pivot_row, both - both[:, k : k + 1] * pivot_row)
    return both[:, n:]


MESH = pl.DeviceIdType.MESH


def others(axes, stop=None):
    size, me = 1, 0
    for name, n in axes:
        size, me = size * n, me * n + lax.axis_index(name)
    found = []
    for d in range(1, stop or size):
        flat = lax.rem(me + d, size)
        where = {}
        for name, n in reversed(axes):
            where[name] = lax.rem(flat, n)
            flat = flat // n
        found.append(where)
    return found


def exchange(targets, source, landing, send_sem, recv_sem):
    copies = []
    for k, where in enumerate(targets):
        copies.append(
            pltpu.make_async_remote_copy(
                src_ref=source(where),
                dst_ref=landing.at[k],
                send_sem=send_sem.at[k],
                recv_sem=recv_sem.at[k],
                device_id=where,
                device_id_type=MESH,
            )
        )
        copies[-1].start()
    return copies


def greet(targets):
    barrier = pltpu.get_barrier_semaphore()
    for where in targets:
        pl.semaphore_signal(barrier, inc=1, device_id=where, device_id_type=MESH)
    pl.semaphore_wait(barrier, len(targets))


def sum_stages(n_row, n_col):
    row, col = ("row", n_row), ("col", n_col)
    return [[row, col]] if n_row * n_col <= 16 else [[row], [col]]


def tail_body(*refs, n_row, n_col):
    homed = refs[: n_col - 1]
    (
        to_row, to_col, noise, sol, res, direction, sol_out, res_out, dir_out,
        land_row, land_col, image, own, land, s_row, r_row, s_col, r_col, s_sum, r_sum,
    ) = refs[n_col - 1 :]
    side = direction.shape[0]
    width = to_row.shape[1]
    stages = sum_stages(n_row, n_col)
    greet([where for axes in stages for where in others(axes)])
    over_row = exchange(
        others([("row", n_row)]), lambda o: to_col.at[o["row"]], land_col, s_col, r_col
    )
    over_col = exchange(
        others([("col", n_col)], 2), lambda o: to_row, land_row, s_row, r_row
    )
    d = direction[...]
    r = res[...]
    gram_res = exact_dot(r, r, 1, 1)
    for copy in over_row:
        copy.wait_recv()
    for copy in over_col:
        copy.wait_recv()
    total = to_col[lax.axis_index("row")] + land_row[0]
    for part in homed:
        total += part[...]
    for k in range(n_row - 1):
        total += land_col[k]
    for b in range(BLK_DEV):
        at = slice(b * width, (b + 1) * width)
        shift = noise[:, at] + total[BLK_DEV * side + b : BLK_DEV * side + b + 1]
        image[:, at] = shift * d[:, at] + total[b * side : (b + 1) * side]
    im = image[...]

    def all_sum(turn, value):
        first = 0
        for stage, axes in enumerate(stages):
            mine = own.at[2 * turn + stage]
            mine[...] = value
            targets = others(axes)
            part = pl.ds(first, len(targets))
            copies = exchange(
                targets, lambda o: mine, land.at[turn, part],
                s_sum.at[turn, part], r_sum.at[turn, part],
            )
            for copy in copies:
                copy.wait_recv()
            for k in range(len(targets)):
                value = value + land[turn, first + k]
            first += len(targets)
            waiting.extend(copies)
        return value

    waiting = over_row + over_col
    curv = 0.5 * (exact_dot(d, im, 1, 1) + exact_dot(im, d, 1, 1))
    blank = jnp.zeros((side, 128 - 2 * side), F32)
    sums = all_sum(0, jnp.concatenate([curv, gram_res, blank], 1))
    norms = sums[:, side : 2 * side]
    curv_inv = invert(sums[:, :side])
    norms_inv = invert(norms)
    alpha_t = exact_dot(norms, curv_inv, 1, 0)
    r_next = r - exact_dot(alpha_t, im, 1, 0)
    res_out[...] = r_next
    gram_next = exact_dot(r_next, r_next, 1, 1)
    blank = jnp.zeros((side, 128 - side), F32)
    sol_out[...] = sol[...] + exact_dot(alpha_t, d, 1, 0)
    norms_next = all_sum(1, jnp.concatenate([gram_next, blank], 1))[:, :side]
    beta_t = exact_dot(norms_next, norms_inv, 1, 0)
    dir_out[...] = r_next + exact_dot(beta_t, d, 1, 0)
    for copy in waiting:
        copy.wait_send()


def tail_call(homed, to_row, to_col, noise, sol, res, direction):
    n_col, n_row = len(homed) + 1, to_col.shape[0]
    n_sum = sum(math.prod(n for _, n in axes) - 1 for axes in sum_stages(n_row, n_col))
    side, points = direction.shape
    vmem = pl.BlockSpec(memory_space=pltpu.VMEM)
    shape = jax.ShapeDtypeStruct((side, points), F32)
    dma = pltpu.SemaphoreType.DMA
    return pl.pallas_call(
        functools.partial(tail_body, n_row=n_row, n_col=n_col),
        out_shape=(shape,) * 3,
        in_specs=[vmem] * (6 + len(homed)),
        out_specs=(vmem,) * 3,
        scratch_shapes=[
            pltpu.VMEM((1,) + to_row.shape, F32),
            pltpu.VMEM((n_row - 1,) + to_col.shape[1:], F32),
            pltpu.VMEM((side, points), F32),
            pltpu.VMEM((4, side, 128), F32),
            pltpu.VMEM((2, n_sum, side, 128), F32),
            dma((1,)), dma((1,)),
            dma((n_row - 1,)), dma((n_row - 1,)),
            dma((2, n_sum)), dma((2, n_sum)),
        ],
        compiler_params=pltpu.CompilerParams(
            collective_id=1, has_side_effects=True, vmem_limit_bytes=40 * 2**20
        ),
        name="tail",
    )(*homed, to_row, to_col, noise, sol, res, direction)


def on_device(features, noise, solution, residual, direction, tile_rows, tile_cols, tile_count):
    side = direction.shape[0]
    n_row, n_col = lax.axis_size("row"), lax.axis_size("col")
    own = jnp.concatenate([features, direction], 0)
    chips = n_row // 2

    def along_x(value):
        return lax.ppermute(value, "row", [(r, (r + 2) % n_row) for r in range(n_row)])

    def between_cores(value):
        return lax.ppermute(value, "row", [(r, r ^ 1) for r in range(n_row)])

    def along_col(value, step):
        return lax.ppermute(value, "col", [(c, (c + step) % n_col) for c in range(n_col)])

    ring = [own]
    for _ in range(n_col - 1):
        ring.append(along_col(ring[-1], 1))
    pieces = [own]
    for _ in range(chips - 1):
        pieces.append(along_x(pieces[-1]))
    pieces += [between_cores(piece) for piece in pieces]
    pairs = tile_rows[0] * (n_row * BLK_DEV) + tile_cols[0]
    right, d_col, slots, totals = prep_call(pairs, tile_count, pieces, side, n_col)
    acc = None
    homed = []
    for p in range(n_col):
        to_row, acc = phase_call(slots, totals, ring[p], right, d_col, acc, p, n_row, n_col)
        if p < n_col - 1:
            homed.append(along_col(to_row, -p) if p else to_row)
    return tail_call(homed, to_row, acc, noise[None, :], solution, residual, direction)


def solution(mesh):
    points = P(None, ("groups", "row", "col"))
    in_specs = (
        points,
        P(("groups", "row", "col")),
        points,
        points,
        points,
        P(("groups", "row"), "col", None),
        P(("groups", "row"), "col", None),
        P(("groups", "row"), "col"),
    )
    return jax.shard_map(
        on_device, mesh=mesh, in_specs=in_specs, out_specs=(points,) * 3, check_vma=False
    )
```

```python
import functools
import math

import jax
import jax.numpy as jnp
from jax import lax
from jax.experimental import pallas as pl
from jax.experimental.pallas import tpu as pltpu
from jax.sharding import PartitionSpec as P

BLK_DEV = 4
DEPTH = 208
STACK = 48

HIGH = lax.Precision.HIGHEST
BF16 = jnp.bfloat16
F32 = jnp.float32

CUT = 0.25 ** 0.2
TOP = 5.0 * CUT**4
EDGE = 1.0 / CUT


def parts3(x):
    high = x.astype(BF16).astype(F32)
    rest = x - high
    mid = rest.astype(BF16).astype(F32)
    return high, mid, (rest - mid).astype(BF16).astype(F32)


def stack_features(x, left):
    width = x.shape[1]
    norm = jnp.sum(x * x, 0, keepdims=True)
    high, mid, low = parts3(x)
    n_high, n_mid, n_low = parts3(norm)
    ones = jnp.ones((1, width), F32)
    zero = jnp.zeros((2, width), F32)
    if left:
        rows = [high, high, mid, mid, high, low]
        rows += [jnp.concatenate([n_high, n_mid, n_low, ones, ones, ones, zero], 0)]
    else:
        high, mid, low = -2.0 * high, -2.0 * mid, -2.0 * low
        rows = [high, mid, high, mid, low, high]
        rows += [jnp.concatenate([ones, ones, ones, n_high, n_mid, n_low, zero], 0)]
    used = sum(r.shape[0] for r in rows)
    rows += [jnp.zeros((DEPTH - used, width), F32)]
    return jnp.concatenate(rows, 0)


def stack_directions(d):
    high = d.astype(BF16)
    low = (d - high.astype(F32)).astype(BF16)
    return jnp.concatenate([high, low, jnp.ones_like(high)], 0)


def dot(a, b, ca, cb):
    return lax.dot_general(a, b, (((ca,), (cb,)), ((), ())), preferred_element_type=F32)


def prep_body(pairs_ref, count_ref, *refs, n_row, n_col):
    pieces, (right, d_col, slots, totals) = refs[:n_row], refs[n_row:]
    width = right.shape[2]
    feat = pieces[0].shape[0] - d_col.shape[1] // 3
    scale = EDGE / (1.5 * math.sqrt(feat))
    me = lax.axis_index("row")
    col = lax.axis_index("col")
    for p in range(n_col):
        totals[p] = 0

    def sort(t, _):
        pair = pairs_ref[0, t]
        p = lax.rem(col - pair // (n_row * BLK_DEV * BLK_DEV) + n_col, n_col)
        at = totals[p]
        slots[p, at] = pair
        totals[p] = at + 1
        return 0

    lax.fori_loop(0, count_ref[0, 0], sort, 0)
    for k, piece in enumerate(pieces):
        core = lax.rem(me, 2) if k < n_row // 2 else 1 - lax.rem(me, 2)
        place = lax.rem(me // 2 - k % (n_row // 2) + n_row // 2, n_row // 2)
        first = (2 * place + core) * BLK_DEV
        for b in range(BLK_DEV):
            at = slice(b * width, (b + 1) * width)
            right[first + b] = stack_features(piece[:feat, at] * scale, False).astype(BF16)
            d_col[first + b] = stack_directions(piece[feat:, at])


def prep_call(pairs, count, pieces, side, n_col):
    n_row = len(pieces)
    width = pieces[0].shape[1] // BLK_DEV
    smem = pl.BlockSpec(memory_space=pltpu.SMEM)
    vmem = pl.BlockSpec(memory_space=pltpu.VMEM)
    return pl.pallas_call(
        functools.partial(prep_body, n_row=n_row, n_col=n_col),
        out_shape=(
            jax.ShapeDtypeStruct((n_row * BLK_DEV, DEPTH, width), BF16),
            jax.ShapeDtypeStruct((n_row * BLK_DEV, 3 * side, width), BF16),
            jax.ShapeDtypeStruct((n_col, pairs.shape[1]), jnp.int32),
            jax.ShapeDtypeStruct((n_col,), jnp.int32),
        ),
        in_specs=[smem] * 2 + [vmem] * n_row,
        out_specs=(vmem, vmem, smem, smem),
        compiler_params=pltpu.CompilerParams(vmem_limit_bytes=40 * 2**20),
        cost_estimate=pl.CostEstimate(
            flops=2 * 10**9, bytes_accessed=8 * 2**20, transcendentals=0
        ),
        name="prep",
    )(pairs, count, *pieces)


def phase_body(slots, totals, piece, right, d_col, *refs, phase, n_row, n_col):
    first, last = phase == 0, phase == n_col - 1
    acc_in = None if first else refs[0]
    to_row, to_col, left, d_row, acc_row, held_a, held_b = refs[0 if first else 1 :][:7]
    acc_col = refs[-1] if last else to_col
    width = right.shape[2]
    side = d_col.shape[1] // 3
    feat = piece.shape[0] - side
    scale = EDGE / (1.5 * math.sqrt(feat))
    n_blocks = n_row * BLK_DEV
    rank_row = lax.axis_index("row")
    rank_col = lax.axis_index("col")
    owner = lax.rem(rank_col - phase + n_col, n_col)
    span = n_col * BLK_DEV
    for b in range(BLK_DEV):
        at = slice(b * width, (b + 1) * width)
        left[b] = stack_features(piece[:feat, at] * scale, True).T.astype(BF16)
        d_row[b] = stack_directions(piece[feat:, at])
    acc_row[...] = jnp.zeros_like(acc_row)

    def carry_over(b, _):
        acc_col[b] = jnp.zeros(acc_col.shape[1:], F32) if first else acc_in[b]
        return 0

    lax.fori_loop(0, n_blocks, carry_over, 0)

    count = totals[phase]

    def place(t):
        pair = slots[phase, t]
        i = pair // n_blocks
        return i, lax.rem(pair, n_blocks)

    def evaluate(t, held):
        i, j = place(t)
        dist = jnp.maximum(dot(left[i - owner * BLK_DEV], right[j], 1, 0), 1e-30)
        v = jnp.maximum(EDGE - dist * lax.rsqrt(dist), 0.0)
        v2 = v * v
        held[...] = (v2 * v2 * (TOP - v)).astype(BF16)

    def multiply(t, held, used):
        i, j = place(t)
        big_i = rank_row * span + i
        big_j = j // BLK_DEV * span + rank_col * BLK_DEV + j % BLK_DEV
        mirror = (big_i != big_j).astype(F32) * used
        i = i - owner * BLK_DEV
        kern = held[...]
        into_row = dot(d_col[j], kern, 1, 1) * used
        into_col = dot(d_row[i], kern, 1, 0) * mirror
        acc_row[i] += into_row
        acc_col[j] += into_col

    def two_tiles(pair_at, _):
        t = 2 * pair_at
        second = jnp.minimum(t + 1, count - 1)
        evaluate(second, held_b)
        multiply(t, held_a, 1.0)
        evaluate(jnp.minimum(t + 2, count - 1), held_a)
        multiply(second, held_b, (t + 1 < count).astype(F32))
        return 0

    @pl.when(count > 0)
    def _():
        evaluate(0, held_a)
        lax.fori_loop(0, (count + 1) // 2, two_tiles, 0)

    def finish(acc, owner_at, out):
        degrees = []
        for b in range(BLK_DEV):
            whole = acc[owner_at * BLK_DEV + b]
            out[b * side : (b + 1) * side] = whole[:side] + whole[side : 2 * side]
            degrees.append(whole[2 * side : 2 * side + 1])
        degrees.append(jnp.zeros((8 - BLK_DEV, width), F32))
        out[BLK_DEV * side :] = jnp.concatenate(degrees, 0)

    finish(acc_row, 0, to_row)
    if last:

        def one(o, _):
            finish(acc_col, o, to_col.at[o])
            return 0

        lax.fori_loop(0, n_row, one, 0)


def phase_call(slots, totals, piece, right, d_col, acc, phase, n_row, n_col):
    width = right.shape[2]
    stack = d_col.shape[1]
    side = stack // 3
    first, last = phase == 0, phase == n_col - 1
    smem = pl.BlockSpec(memory_space=pltpu.SMEM)
    vmem = pl.BlockSpec(memory_space=pltpu.VMEM)
    packed = (BLK_DEV * side + 8, width)
    sums = (n_row * BLK_DEV, stack, width)
    scratch = [
        pltpu.VMEM((BLK_DEV, width, DEPTH), BF16),
        pltpu.VMEM((BLK_DEV, stack, width), BF16),
        pltpu.VMEM((BLK_DEV, stack, width), F32),
        pltpu.VMEM((width, width), BF16),
        pltpu.VMEM((width, width), BF16),
    ]
    if last:
        scratch.append(pltpu.VMEM(sums, F32))
    accs = () if first else (acc,)
    return pl.pallas_call(
        functools.partial(phase_body, phase=phase, n_row=n_row, n_col=n_col),
        out_shape=(
            jax.ShapeDtypeStruct(packed, F32),
            jax.ShapeDtypeStruct((n_row,) + packed if last else sums, F32),
        ),
        in_specs=[smem] * 2 + [vmem] * (3 + len(accs)),
        out_specs=(vmem, vmem),
        scratch_shapes=scratch,
        compiler_params=pltpu.CompilerParams(vmem_limit_bytes=36 * 2**20),
        cost_estimate=pl.CostEstimate(
            flops=14 * 10**9, bytes_accessed=8 * 2**20, transcendentals=0
        ),
        name=f"phase{phase}",
    )(slots, totals, piece, right, d_col, *accs)


def exact_dot(a, b, ca, cb):
    return lax.dot_general(
        a, b, (((ca,), (cb,)), ((), ())), precision=HIGH, preferred_element_type=F32
    )


def invert(matrix):
    n = matrix.shape[0]
    rows = lax.broadcasted_iota(jnp.int32, (n, n), 0)
    cols = lax.broadcasted_iota(jnp.int32, (n, n), 1)
    both = jnp.concatenate([matrix, (rows == cols).astype(F32)], 1)
    at = lax.broadcasted_iota(jnp.int32, both.shape, 0)
    for k in range(n):
        pivot_row = both[k : k + 1, :] / both[k : k + 1, k : k + 1]
        both = jnp.where(at == k, pivot_row, both - both[:, k : k + 1] * pivot_row)
    return both[:, n:]


MESH = pl.DeviceIdType.MESH


def others(axes, stop=None):
    size, me = 1, 0
    for name, n in axes:
        size, me = size * n, me * n + lax.axis_index(name)
    found = []
    for d in range(1, stop or size):
        flat = lax.rem(me + d, size)
        where = {}
        for name, n in reversed(axes):
            where[name] = lax.rem(flat, n)
            flat = flat // n
        found.append(where)
    return found


def exchange(targets, source, landing, send_sem, recv_sem):
    copies = []
    for k, where in enumerate(targets):
        copies.append(
            pltpu.make_async_remote_copy(
                src_ref=source(where),
                dst_ref=landing.at[k],
                send_sem=send_sem.at[k],
                recv_sem=recv_sem.at[k],
                device_id=where,
                device_id_type=MESH,
            )
        )
        copies[-1].start()
    return copies


def greet(targets):
    barrier = pltpu.get_barrier_semaphore()
    for where in targets:
        pl.semaphore_signal(barrier, inc=1, device_id=where, device_id_type=MESH)
    pl.semaphore_wait(barrier, len(targets))


def sum_stages(n_row, n_col):
    row, col = ("row", n_row), ("col", n_col)
    return [[row, col]] if n_row * n_col <= 16 else [[row], [col]]


def tail_body(*refs, n_row, n_col):
    homed = refs[: n_col - 1]
    (
        to_row, to_col, noise, sol, res, direction, sol_out, res_out, dir_out,
        land_row, land_col, image, own, land, s_row, r_row, s_col, r_col, s_sum, r_sum,
    ) = refs[n_col - 1 :]
    side = direction.shape[0]
    width = to_row.shape[1]
    stages = sum_stages(n_row, n_col)
    greet([where for axes in stages for where in others(axes)])
    over_row = exchange(
        others([("row", n_row)]), lambda o: to_col.at[o["row"]], land_col, s_col, r_col
    )
    over_col = exchange(
        others([("col", n_col)], 2), lambda o: to_row, land_row, s_row, r_row
    )
    d = direction[...]
    r = res[...]
    gram_res = exact_dot(r, r, 1, 1)
    for copy in over_row:
        copy.wait_recv()
    for copy in over_col:
        copy.wait_recv()
    total = to_col[lax.axis_index("row")] + land_row[0]
    for part in homed:
        total += part[...]
    for k in range(n_row - 1):
        total += land_col[k]
    for b in range(BLK_DEV):
        at = slice(b * width, (b + 1) * width)
        shift = noise[:, at] + total[BLK_DEV * side + b : BLK_DEV * side + b + 1]
        image[:, at] = shift * d[:, at] + total[b * side : (b + 1) * side]
    im = image[...]

    def all_sum(turn, value):
        first = 0
        for stage, axes in enumerate(stages):
            mine = own.at[2 * turn + stage]
            mine[...] = value
            targets = others(axes)
            part = pl.ds(first, len(targets))
            copies = exchange(
                targets, lambda o: mine, land.at[turn, part],
                s_sum.at[turn, part], r_sum.at[turn, part],
            )
            for copy in copies:
                copy.wait_recv()
            for k in range(len(targets)):
                value = value + land[turn, first + k]
            first += len(targets)
            waiting.extend(copies)
        return value

    waiting = over_row + over_col
    curv = 0.5 * (exact_dot(d, im, 1, 1) + exact_dot(im, d, 1, 1))
    blank = jnp.zeros((side, 128 - 2 * side), F32)
    sums = all_sum(0, jnp.concatenate([curv, gram_res, blank], 1))
    norms = sums[:, side : 2 * side]
    curv_inv = invert(sums[:, :side])
    norms_inv = invert(norms)
    alpha_t = exact_dot(norms, curv_inv, 1, 0)
    r_next = r - exact_dot(alpha_t, im, 1, 0)
    res_out[...] = r_next
    gram_next = exact_dot(r_next, r_next, 1, 1)
    blank = jnp.zeros((side, 128 - side), F32)
    sol_out[...] = sol[...] + exact_dot(alpha_t, d, 1, 0)
    norms_next = all_sum(1, jnp.concatenate([gram_next, blank], 1))[:, :side]
    beta_t = exact_dot(norms_next, norms_inv, 1, 0)
    dir_out[...] = r_next + exact_dot(beta_t, d, 1, 0)
    for copy in waiting:
        copy.wait_send()


def tail_call(homed, to_row, to_col, noise, sol, res, direction):
    n_col, n_row = len(homed) + 1, to_col.shape[0]
    n_sum = sum(math.prod(n for _, n in axes) - 1 for axes in sum_stages(n_row, n_col))
    side, points = direction.shape
    vmem = pl.BlockSpec(memory_space=pltpu.VMEM)
    shape = jax.ShapeDtypeStruct((side, points), F32)
    dma = pltpu.SemaphoreType.DMA
    return pl.pallas_call(
        functools.partial(tail_body, n_row=n_row, n_col=n_col),
        out_shape=(shape,) * 3,
        in_specs=[vmem] * (6 + len(homed)),
        out_specs=(vmem,) * 3,
        scratch_shapes=[
            pltpu.VMEM((1,) + to_row.shape, F32),
            pltpu.VMEM((n_row - 1,) + to_col.shape[1:], F32),
            pltpu.VMEM((side, points), F32),
            pltpu.VMEM((4, side, 128), F32),
            pltpu.VMEM((2, n_sum, side, 128), F32),
            dma((1,)), dma((1,)),
            dma((n_row - 1,)), dma((n_row - 1,)),
            dma((2, n_sum)), dma((2, n_sum)),
        ],
        compiler_params=pltpu.CompilerParams(
            collective_id=1, has_side_effects=True, vmem_limit_bytes=40 * 2**20
        ),
        name="tail",
    )(*homed, to_row, to_col, noise, sol, res, direction)


def on_device(features, noise, solution, residual, direction, tile_rows, tile_cols, tile_count):
    side = direction.shape[0]
    n_row, n_col = lax.axis_size("row"), lax.axis_size("col")
    own = jnp.concatenate([features, direction], 0)
    chips = n_row // 2

    def along_x(value):
        return lax.ppermute(value, "row", [(r, (r + 2) % n_row) for r in range(n_row)])

    def between_cores(value):
        return lax.ppermute(value, "row", [(r, r ^ 1) for r in range(n_row)])

    def along_col(value, step):
        return lax.ppermute(value, "col", [(c, (c + step) % n_col) for c in range(n_col)])

    ring = [own]
    for _ in range(n_col - 1):
        ring.append(along_col(ring[-1], 1))
    pieces = [own]
    for _ in range(chips - 1):
        pieces.append(along_x(pieces[-1]))
    pieces += [between_cores(piece) for piece in pieces]
    pairs = tile_rows[0] * (n_row * BLK_DEV) + tile_cols[0]
    right, d_col, slots, totals = prep_call(pairs, tile_count, pieces, side, n_col)
    acc = None
    homed = []
    for p in range(n_col):
        if 0 < p < n_col - 1:
            acc, ring[p + 1] = lax.optimization_barrier((acc, ring[p + 1]))
        to_row, acc = phase_call(slots, totals, ring[p], right, d_col, acc, p, n_row, n_col)
        if p < n_col - 1:
            homed.append(along_col(to_row, -p) if p else to_row)
    return tail_call(homed, to_row, acc, noise[None, :], solution, residual, direction)


def solution(mesh):
    points = P(None, ("groups", "row", "col"))
    in_specs = (
        points,
        P(("groups", "row", "col")),
        points,
        points,
        points,
        P(("groups", "row"), "col", None),
        P(("groups", "row"), "col", None),
        P(("groups", "row"), "col"),
    )
    return jax.shard_map(
        on_device, mesh=mesh, in_specs=in_specs, out_specs=(points,) * 3, check_vma=False
    )
```
